512 devices in a mesh: grp: 16 (over x, z_hi, core), ctx: 32 (over y, z_lo).
Axes of the slice: x: 4, y: 8, z: 8 (z_hi: 2, z_lo: 4; z = z_hi * 4 + z_lo), core: 2. Of those that a mesh axis runs over, the one named last changes fastest.
Arguments:
- queries: bfloat16 [32768, 4096], P(('grp', 'ctx')), may hold values from -200 to 200
- key_rows: bfloat16 [32768, 512], P(('grp', 'ctx')), may hold values from -10 to 10
- value_rows: bfloat16 [32768, 512], P(('grp', 'ctx')), may hold values from -6 to 6
- doc_ids: int32 [16, 2048], P('grp', 'ctx'), may hold values from 0 to 5, never falling along the last dimension, each value on 1 to 1024 neighbouring positions
Outputs:
- attended: bfloat16 [32768, 4096], P(('grp', 'ctx'))
- log_totals: float32 [32, 32768], P(None, ('grp', 'ctx'))
The draws below stay inside these ranges and needn't reach their ends.
Inputs may be any that keep to these rules, and one draw needn't show every extreme that they name: `doc_ids`: nondecreasing along each group's tokens; every prompt has 1 to 1024 tokens and one has exactly 1024.
All inputs are finite; a program needn't handle non-finite values.
Results may differ from the reference program's by a relative error of at most 0.0065.
Values may be sent and summed in bfloat16 or wider, within the bound.
No kernel may reach another device: no remote copies, remote signals or barrier semaphores. Data moves between devices by JAX's collectives and lax.ppermute only.
A program may use at most 64 MiB of HBM per device.

```python
import math
import jax
import jax.numpy as jnp
import numpy as np
from jax import lax

QH = 32
KVH = 4
DH = 128
COUNT = 6
GLEN = 2048
MOST = 1024
TOKENS = 32768
N_GRP = 16


def shared_rows(key, weight):
    key_base = jax.random.normal(jax.random.fold_in(key, 101), (TOKENS, KVH, DH), jnp.float32)
    chosen = (jax.random.uniform(jax.random.fold_in(key, 102), (TOKENS,)) < 1.0 / 64.0) & (jnp.arange(TOKENS) > 0)
    return (key_base, chosen.astype(jnp.float32) * weight)


def draw_key_rows(key, part):
    weight = 0.0
    key_base, chosen = shared_rows(key, weight)
    key = jax.random.fold_in(key, 3)
    jitter = 0.1 * jax.random.normal(key, (TOKENS, KVH, DH), jnp.float32)
    ahead_rows = jnp.roll(key_base, -1, 0)
    chosen_ahead = jnp.roll(chosen, -1)
    result = key_base + chosen_ahead[:, None, None] * (ahead_rows + jitter - key_base)
    return result.reshape(TOKENS, KVH * DH).astype(jnp.bfloat16)


def draw_queries(key, part):
    key = jax.random.fold_in(key, 5)
    fresh_rows = jax.random.normal(key, (TOKENS, KVH, QH // KVH, DH), jnp.float32)
    result = fresh_rows
    return result.reshape(TOKENS, QH * DH).astype(jnp.bfloat16)


def block_levels(stream_key, extent, split, least, top_value):
    gain = 1.0
    for position, shards_of in split:
        heights = jax.random.uniform(jax.random.fold_in(jax.random.fold_in(stream_key, 6), position), (shards_of,), jnp.float32, least / len(split), top_value / len(split))
        gain = gain * jnp.repeat(jnp.exp(heights), extent[position] // shards_of).reshape((-1,) + (1,) * (len(extent) - 1 - position))
    return gain


def length_profile(count, total, most, slope):
    loads = [(1 << 20) // math.isqrt(grade ** slope) + 1 for grade in range(2, count + 1)]
    surplus, counts = total - most - (count - 1), [1] * (count - 1)
    while surplus > 0:
        free = [i for i in range(count - 1) if counts[i] < most]
        mass, budget = sum([loads[i] for i in free]), surplus
        for i in free:
            more = min(most - counts[i], max(1, budget * loads[i] // mass), surplus)
            counts[i] = counts[i] + more
            surplus = surplus - more
    return np.array([most] + counts)


def uneven_parts(own_key, amount, total, limit, slope):
    if amount == 2:
        one = jax.random.randint(own_key, (), max(1, total - limit), min(limit, total - 1) + 1)
        return jnp.stack([one, total - one])
    lengths = jnp.asarray(length_profile(amount, total, limit, slope), jnp.int32)
    pairs = (amount - 1) // 2
    donor, receiver = lengths[1:1 + 2 * pairs:2], lengths[2:2 + 2 * pairs:2]
    room = jnp.minimum(donor - 1, limit - receiver)
    moved = jax.random.randint(jax.random.fold_in(own_key, 1), (pairs,), 0, 1 << 20) % (room + 1)
    lengths = lengths.at[1:1 + 2 * pairs:2].set(donor - moved).at[2:2 + 2 * pairs:2].set(receiver + moved)
    return lengths[jax.random.permutation(jax.random.fold_in(own_key, 2), amount)]


def noise(rng, dims, spread, reach, cuts=(), held_as=jnp.bfloat16):
    values = jax.random.normal(rng, dims, jnp.float32) * spread
    if len(cuts) > 0:
        values = block_levels(rng, dims, cuts, -0.22, 0.18) * values
    return jnp.clip(values, min=-reach, max=reach).astype(held_as)


def setup_inputs(seed: int = 0) -> dict:
    arg_keys = jax.random.split(jax.random.key(seed), 5)
    queries = draw_queries(jax.random.fold_in(arg_keys[4], 71), 0)
    key_rows = draw_key_rows(jax.random.fold_in(arg_keys[4], 71), 0)
    value_rows = noise(arg_keys[2], (TOKENS, KVH * DH), 1.0, 6.0, ((0, 512),))
    doc_ids = jax.vmap(lambda own: jnp.searchsorted(jnp.cumsum(uneven_parts(own, COUNT, GLEN, MOST, 2)), jnp.arange(GLEN), side="right"))(jax.random.split(arg_keys[3], N_GRP)).reshape((N_GRP, GLEN)).astype(jnp.int32)
    return {"queries": queries, "key_rows": key_rows, "value_rows": value_rows, "doc_ids": doc_ids}


def reference(queries, key_rows, value_rows, doc_ids):
    ratio = QH // KVH
    block = min(512, GLEN)
    score_scale = 1.0 / (DH ** 0.5)
    query_groups = queries.reshape(N_GRP, GLEN, KVH, ratio, DH)
    key_groups = key_rows.reshape(N_GRP, GLEN, KVH, DH)
    value_groups = value_rows.reshape(N_GRP, GLEN, KVH, DH)

    def one_group(items):
        query_all, key_all, value_all, doc_row = items
        pieces = []
        log_pieces = []
        for block_index in range(GLEN // block):
            first_row = block_index * block
            last_row = first_row + block
            query_block = jnp.moveaxis(query_all[first_row:last_row], 1, 0)
            key_block = jnp.moveaxis(key_all[:last_row], 1, 0)
            value_block = jnp.moveaxis(value_all[:last_row], 1, 0)
            query_pos = jnp.arange(first_row, last_row).astype(jnp.int32)
            key_pos = jnp.arange(last_row).astype(jnp.int32)
            allowed = (key_pos[None, :] <= query_pos[:, None]) & (doc_row[None, :last_row] == doc_row[first_row:last_row, None])

            def per_head(heads):
                query_head, key_head, value_head = heads
                scores = jnp.einsum("tgd,pd->gtp", query_head.astype(jnp.float32), key_head.astype(jnp.float32)) * score_scale
                masked = jnp.where(allowed[None], scores, -1e30)
                row_max = jnp.max(masked, axis=-1)
                weights = jnp.where(allowed[None], jnp.exp(scores - row_max[..., None]), 0.0)
                denominator = jnp.sum(weights, axis=-1)
                rounded = weights.astype(jnp.bfloat16)
                mixed = jnp.einsum("gtp,pd->gtd", rounded.astype(jnp.float32), value_head.astype(jnp.float32))
                mixed = mixed / denominator[..., None]
                return mixed.astype(jnp.bfloat16), row_max + jnp.log(denominator)

            mixed, log_block = lax.map(per_head, (query_block, key_block, value_block))
            pieces.append(jnp.transpose(mixed, (2, 0, 1, 3)).reshape(block, QH * DH))
            log_pieces.append(log_block.reshape(QH, block))
        return jnp.concatenate(pieces, 0), jnp.concatenate(log_pieces, 1)

    attended, log_totals = lax.map(one_group, (query_groups, key_groups, value_groups, doc_ids))
    return attended.reshape(TOKENS, QH * DH), jnp.transpose(log_totals, (1, 0, 2)).reshape(QH, TOKENS)
```

```python
import functools
import math

import jax
import jax.numpy as jnp
from jax import lax
from jax.experimental import pallas as pl
from jax.experimental.pallas import tpu as pltpu
from jax.sharding import Mesh, PartitionSpec as P

QH = 32
KVH = 4
DH = 128
RATIO = QH // KVH
ROWS = 8
COLS = 4
MOST = 1024
NEG = -1e30


def attend_kernel(row_ref, q_ref, own_ref, *rest):
    halo_refs = rest[:-3]
    out_ref, bias_ref, value_ref = rest[-3:]
    tokens = q_ref.shape[0]
    chunks = (own_ref,) + tuple(halo_refs)
    row = row_ref[0]
    own_docs = own_ref[tokens:, :].astype(jnp.float32)
    doc_col = own_docs.T[:, :1]
    q_pos = lax.broadcasted_iota(jnp.int32, (tokens, tokens), 0)
    k_pos = lax.broadcasted_iota(jnp.int32, (tokens, tokens), 1)
    for i, chunk in enumerate(chunks):
        doc_row = chunk[tokens:, :].astype(jnp.float32)[:1]
        allowed = doc_col == doc_row
        if i == 0:
            allowed = allowed & (k_pos <= q_pos)
        else:
            allowed = allowed & (row >= i)
        bias_ref[i] = jnp.where(allowed, 0.0, NEG)
        value_ref[i, :, :DH] = chunk[:tokens, DH:]
        value_ref[i, :, DH:] = jnp.ones((tokens, DH), jnp.bfloat16)
    scale = 1.0 / math.sqrt(DH)
    scale2 = scale * math.log2(math.e)
    lanes = lax.broadcasted_iota(jnp.int32, (tokens, DH), 1)
    logs = jnp.zeros((tokens, DH), jnp.float32)
    for head in range(RATIO):
        query = q_ref[:, head * DH : (head + 1) * DH]
        scores = []
        for i, chunk in enumerate(chunks):
            product = lax.dot_general(
                query,
                chunk[:tokens, :DH],
                (((1,), (1,)), ((), ())),
                preferred_element_type=jnp.float32,
            )
            scores.append(product + bias_ref[i])
        top = functools.reduce(jnp.maximum, scores)
        row_max = jnp.max(top, axis=1, keepdims=True)
        total = jnp.zeros((tokens, 2 * DH), jnp.float32)
        for i in range(len(chunks)):
            weights = jnp.exp2((scores[i] - row_max) * scale2).astype(jnp.bfloat16)
            total += jnp.dot(weights, value_ref[i], preferred_element_type=jnp.float32)
        denominator = total[:, DH:]
        out_ref[:, head * DH : (head + 1) * DH] = (total[:, :DH] / denominator).astype(jnp.bfloat16)
        log_total = row_max * scale + jnp.log(denominator)
        high = log_total.astype(jnp.bfloat16).astype(jnp.float32)
        logs = jnp.where(lanes == head, high, logs)
        logs = jnp.where(lanes == RATIO + head, log_total - high, logs)
    out_ref[:, RATIO * DH :] = logs.astype(jnp.bfloat16)


def attend(row, query, own, halo):
    tokens = query.shape[0]
    count = 1 + len(halo)
    whole = pl.BlockSpec(memory_space=pltpu.VMEM)
    return pl.pallas_call(
        attend_kernel,
        out_shape=jax.ShapeDtypeStruct((tokens, (RATIO + 1) * DH), jnp.bfloat16),
        in_specs=[pl.BlockSpec(memory_space=pltpu.SMEM)] + [whole] * (1 + count),
        out_specs=whole,
        scratch_shapes=[
            pltpu.VMEM((count, tokens, tokens), jnp.float32),
            pltpu.VMEM((count, tokens, 2 * DH), jnp.bfloat16),
        ],
        compiler_params=pltpu.CompilerParams(vmem_limit_bytes=48 * 1024 * 1024),
        cost_estimate=pl.CostEstimate(
            flops=4 * RATIO * tokens * tokens * count * DH * 2,
            bytes_accessed=3 * 1024 * 1024,
            transcendentals=RATIO * tokens * tokens * count,
        ),
    )(row, query, own, *halo)


def per_device(queries, key_rows, value_rows, doc_ids):
    count = queries.shape[0]
    tokens = count * COLS
    row = lax.axis_index("y")
    keys = key_rows.reshape(count, KVH, DH)
    values = value_rows.reshape(count, KVH, DH)
    pairs = jnp.transpose(jnp.concatenate([keys, values], 2), (1, 0, 2))
    docs = jnp.pad(doc_ids.astype(jnp.bfloat16), ((0, 15), (0, 2 * DH - count)))
    docs = jnp.broadcast_to(docs[None], (KVH, 16, 2 * DH))
    sent = jnp.concatenate([pairs, docs], 1)
    got = lax.all_to_all(sent, "z", 0, 0, tiled=True)
    doc_line = got[:, count, :count].reshape(1, tokens)
    own = jnp.concatenate(
        [got[:, :count].reshape(tokens, 2 * DH), jnp.broadcast_to(doc_line, (16, tokens))], 0
    )
    halo = []
    for back in range(1, MOST // tokens + 1):
        route = [(low, low + back) for low in range(ROWS - back)]
        halo.append(lax.ppermute(own, "y", route))
    query = jnp.transpose(queries.reshape(count, KVH, RATIO * DH), (1, 0, 2))
    query = lax.all_to_all(query, "z", 0, 0, tiled=True).reshape(tokens, RATIO * DH)
    out = attend(row.reshape(1), query, own, halo)
    back = lax.all_to_all(out.reshape(COLS, count, (RATIO + 1) * DH), "z", 0, 0, tiled=True)
    attended = jnp.transpose(back[:, :, : RATIO * DH], (1, 0, 2)).reshape(count, QH * DH)
    logs = back[:, :, RATIO * DH : RATIO * DH + 2 * RATIO].astype(jnp.float32)
    logs = logs[:, :, :RATIO] + logs[:, :, RATIO:]
    return attended, jnp.transpose(logs, (0, 2, 1)).reshape(QH, count)


def solution(mesh):
    names = ("grp", "y", "z")
    split = Mesh(mesh.devices.reshape(mesh.shape["grp"], ROWS, COLS), names)
    block = P(names, None)
    return jax.shard_map(
        per_device,
        mesh=split,
        in_specs=(block, block, block, P("grp", ("y", "z"))),
        out_specs=(block, P(None, names)),
        check_vma=False,
    )
```

```python
import functools
import math

import jax
import jax.numpy as jnp
from jax import lax
from jax.experimental import pallas as pl
from jax.experimental.pallas import tpu as pltpu
from jax.sharding import Mesh, PartitionSpec as P

QH = 32
KVH = 4
DH = 128
RATIO = QH // KVH
ROWS = 8
COLS = 4
NEG = -1e30
VMEM = pl.BlockSpec(memory_space=pltpu.VMEM)
SMEM = pl.BlockSpec(memory_space=pltpu.SMEM)
ANY = pl.BlockSpec(memory_space=pl.ANY)


def params():
    return pltpu.CompilerParams(vmem_limit_bytes=40 * 1024 * 1024)


def pack_kernel(k_ref, v_ref, doc_ref, out_ref, line_ref, sems):
    count = k_ref.shape[0]
    copies = [pltpu.make_async_copy(doc_ref, line_ref, sems.at[0])]
    for head in range(COLS):
        part = slice(head * DH, (head + 1) * DH)
        for side, ref in enumerate((k_ref, v_ref)):
            target = out_ref.at[head, :count, side * DH : (side + 1) * DH]
            copies.append(pltpu.make_async_copy(ref.at[:, part], target, sems.at[1 + 2 * head + side]))
    for copy in copies:
        copy.start()
    copies[0].wait()
    docs = jnp.broadcast_to(line_ref[...].astype(jnp.float32), (16, count)).astype(jnp.bfloat16)
    for head in range(COLS):
        out_ref[head, count:, :] = jnp.zeros((16, 2 * DH), jnp.bfloat16)
        out_ref[head, count:, :count] = docs
    for copy in copies[1:]:
        copy.wait()


def pack(key_rows, value_rows, doc_ids):
    count = key_rows.shape[0]
    return pl.pallas_call(
        pack_kernel,
        out_shape=jax.ShapeDtypeStruct((COLS, count + 16, 2 * DH), jnp.bfloat16),
        in_specs=[ANY, ANY, ANY],
        out_specs=VMEM,
        scratch_shapes=[
            pltpu.VMEM(doc_ids.shape, doc_ids.dtype),
            pltpu.SemaphoreType.DMA((1 + 2 * COLS,)),
        ],
        compiler_params=pltpu.CompilerParams(vmem_limit_bytes=63 * 1024 * 1024),
    )(key_rows, value_rows, doc_ids)


def attend_kernel(row_ref, q_ref, *refs):
    out_ref, bias_ref, value_ref = refs[-3:]
    chunks = refs[:-3]
    count = q_ref.shape[1]
    tokens = count * COLS
    row = row_ref[0]
    doc_col = chunks[0][tokens:, :].astype(jnp.float32).T[:, :1]
    q_pos = lax.broadcasted_iota(jnp.int32, (tokens, tokens), 0)
    k_pos = lax.broadcasted_iota(jnp.int32, (tokens, tokens), 1)
    for i, chunk in enumerate(chunks):
        doc_row = chunk[tokens:, :].astype(jnp.float32)[:1]
        allowed = doc_col == doc_row
        if i == 0:
            allowed = allowed & (k_pos <= q_pos)
        else:
            allowed = allowed & (row >= i)
        bias_ref[i] = jnp.where(allowed, 0.0, NEG)
        value_ref[i, :, :DH] = chunk[:tokens, DH:]
        value_ref[i, :, DH:] = jnp.ones((tokens, DH), jnp.bfloat16)
    scale = 1.0 / math.sqrt(DH)
    scale2 = scale * math.log2(math.e)
    lanes = lax.broadcasted_iota(jnp.int32, (tokens, DH), 1)
    logs = jnp.zeros((tokens, DH), jnp.float32)
    for head in range(RATIO):
        part = slice(head * DH, (head + 1) * DH)
        query = q_ref[:, :, part].reshape(tokens, DH)
        scores = []
        for i, chunk in enumerate(chunks):
            product = lax.dot_general(
                query,
                chunk[:tokens, :DH],
                (((1,), (1,)), ((), ())),
                preferred_element_type=jnp.float32,
            )
            scores.append(product + bias_ref[i])
        top = functools.reduce(jnp.maximum, scores)
        row_max = jnp.max(top, axis=1, keepdims=True)
        total = jnp.zeros((tokens, 2 * DH), jnp.float32)
        for i in range(len(chunks)):
            weights = jnp.exp2((scores[i] - row_max) * scale2).astype(jnp.bfloat16)
            total += jnp.dot(weights, value_ref[i], preferred_element_type=jnp.float32)
        denominator = total[:, DH:]
        mixed = (total[:, :DH] / denominator).astype(jnp.bfloat16)
        out_ref[:, head * count : (head + 1) * count, :] = mixed.reshape(COLS, count, DH)
        log_total = row_max * scale + jnp.log(denominator)
        high = log_total.astype(jnp.bfloat16).astype(jnp.float32)
        logs = jnp.where(lanes == head, high, logs)
        logs = jnp.where(lanes == RATIO + head, log_total - high, logs)
    logs = logs.T[: 2 * RATIO]
    for step in range(COLS):
        piece = logs[:, step * count : (step + 1) * count]
        piece = jnp.concatenate([piece, piece], 1).astype(jnp.bfloat16)
        out_ref[step, RATIO * count :, :] = piece


def attend(row, query, chunks):
    count = query.shape[1]
    tokens = count * COLS
    return pl.pallas_call(
        attend_kernel,
        out_shape=jax.ShapeDtypeStruct((COLS, RATIO * count + 2 * RATIO, DH), jnp.bfloat16),
        in_specs=[SMEM] + [VMEM] * (1 + len(chunks)),
        out_specs=VMEM,
        scratch_shapes=[
            pltpu.VMEM((len(chunks), tokens, tokens), jnp.float32),
            pltpu.VMEM((len(chunks), tokens, 2 * DH), jnp.bfloat16),
        ],
        compiler_params=params(),
    )(row, query, *chunks)


def join_kernel(in_ref, out_ref, log_ref):
    count = out_ref.shape[0]
    for home in range(COLS):
        for head in range(RATIO):
            first = (home * RATIO + head) * DH
            out_ref[:, first : first + DH] = in_ref[home, head * count : (head + 1) * count, :]
        logs = in_ref[home, RATIO * count :, :].astype(jnp.float32)
        logs = logs[:RATIO] + logs[RATIO:]
        log_ref[home * RATIO : (home + 1) * RATIO, :] = logs[:, :count]


def join(blocks, count):
    return pl.pallas_call(
        join_kernel,
        out_shape=[
            jax.ShapeDtypeStruct((count, QH * DH), jnp.bfloat16),
            jax.ShapeDtypeStruct((QH, count), jnp.float32),
        ],
        in_specs=[VMEM],
        out_specs=[VMEM] * 2,
        compiler_params=params(),
    )(blocks)


def per_device(queries, key_rows, value_rows, doc_ids):
    count = queries.shape[0]
    row = lax.axis_index("y").astype(jnp.int32)
    got = lax.all_to_all(pack(key_rows, value_rows, doc_ids), "z", 0, 0, tiled=True)
    own = jnp.concatenate(
        [piece[:count] for piece in got]
        + [jnp.concatenate([piece[count:, :count] for piece in got], 1)],
        0,
    )

    def ahead(array, back, least=0):
        return lax.ppermute(array, "y", [(i, i + back) for i in range(least, ROWS - back)])

    far = lax.ppermute(own, "y", [(i, (i + 6) % ROWS) for i in range(4)])
    chunks = [own] + [ahead(own, back) for back in (1, 2)]
    chunks.append(ahead(chunks[2], 1, 2))
    far = lax.ppermute(far, "y", [((i + 6) % ROWS, i + 4) for i in range(4)])
    chunks.append(far)

    query = jnp.transpose(queries.reshape(count, COLS, RATIO * DH), (1, 0, 2))
    query = lax.all_to_all(query, "z", 0, 0, tiled=True)
    blocks = attend(row.reshape(1), query, chunks)
    blocks = lax.all_to_all(blocks, "z", 0, 0, tiled=True)
    attended, log_totals = join(blocks, count)
    return attended, log_totals


def solution(mesh):
    names = ("grp", "y", "z")
    split_mesh = Mesh(mesh.devices.reshape(mesh.shape["grp"], ROWS, COLS), names)
    block = P(names, None)
    return jax.shard_map(
        per_device,
        mesh=split_mesh,
        in_specs=(block, block, block, P("grp", ("y", "z"))),
        out_specs=(block, P(None, names)),
        check_vma=False,
    )
```

```python
import functools
import math

import jax
import jax.numpy as jnp
from jax import lax
from jax.experimental import pallas as pl
from jax.experimental.pallas import tpu as pltpu
from jax.sharding import Mesh, PartitionSpec as P

QH = 32
KVH = 4
DH = 128
RATIO = QH // KVH
ROWS = 8
COLS = 4
NEG = -1e30
SCALE = 1.0 / math.sqrt(DH)
SCALE2 = SCALE * math.log2(math.e)
VMEM = pl.BlockSpec(memory_space=pltpu.VMEM)
SMEM = pl.BlockSpec(memory_space=pltpu.SMEM)
ANY = pl.BlockSpec(memory_space=pl.ANY)


def params():
    return pltpu.CompilerParams(vmem_limit_bytes=40 * 1024 * 1024)


def pack_kernel(k_ref, v_ref, doc_ref, out_ref, line_ref, sems):
    count = k_ref.shape[0]
    copies = [pltpu.make_async_copy(doc_ref, line_ref, sems.at[0])]
    for head in range(COLS):
        part = slice(head * DH, (head + 1) * DH)
        for side, ref in enumerate((k_ref, v_ref)):
            target = out_ref.at[head, :count, side * DH : (side + 1) * DH]
            copies.append(pltpu.make_async_copy(ref.at[:, part], target, sems.at[1 + 2 * head + side]))
    for copy in copies:
        copy.start()
    copies[0].wait()
    docs = jnp.broadcast_to(line_ref[...].astype(jnp.float32), (16, count)).astype(jnp.bfloat16)
    for head in range(COLS):
        out_ref[head, count:, :] = jnp.zeros((16, 2 * DH), jnp.bfloat16)
        out_ref[head, count:, :count] = docs
    for copy in copies[1:]:
        copy.wait()


def pack(key_rows, value_rows, doc_ids):
    count = key_rows.shape[0]
    return pl.pallas_call(
        pack_kernel,
        out_shape=jax.ShapeDtypeStruct((COLS, count + 16, 2 * DH), jnp.bfloat16),
        in_specs=[ANY, ANY, ANY],
        out_specs=VMEM,
        scratch_shapes=[
            pltpu.VMEM(doc_ids.shape, doc_ids.dtype),
            pltpu.SemaphoreType.DMA((1 + 2 * COLS,)),
        ],
        compiler_params=pltpu.CompilerParams(vmem_limit_bytes=63 * 1024 * 1024),
    )(key_rows, value_rows, doc_ids)


def write_masks(row, own, chunks, bias_ref, value_ref):
    tokens = bias_ref.shape[1]
    doc_col = own[tokens:, :].astype(jnp.float32).T[:, :1]
    for i, (back, chunk) in enumerate(chunks):
        doc_row = chunk[tokens:, :].astype(jnp.float32)[:1]
        allowed = doc_col == doc_row
        if back == 0:
            q_pos = lax.broadcasted_iota(jnp.int32, (tokens, tokens), 0)
            k_pos = lax.broadcasted_iota(jnp.int32, (tokens, tokens), 1)
            allowed = allowed & (k_pos <= q_pos)
        else:
            allowed = allowed & (row >= back)
        bias_ref[i] = jnp.where(allowed, 0.0, NEG)
        value_ref[i, :, :DH] = chunk[:tokens, DH:]
        value_ref[i, :, DH:] = jnp.ones((tokens, DH), jnp.bfloat16)


def masked_scores(q_ref, head, chunks, bias_ref):
    tokens = bias_ref.shape[1]
    query = q_ref[:, :, head * DH : (head + 1) * DH].reshape(tokens, DH)
    scores = []
    for i, (_, chunk) in enumerate(chunks):
        product = lax.dot_general(
            query, chunk[:tokens, :DH], (((1,), (1,)), ((), ())), preferred_element_type=jnp.float32
        )
        scores.append(product + bias_ref[i])
    return scores, jnp.max(functools.reduce(jnp.maximum, scores), axis=1, keepdims=True)


def weighted(scores, row_max, value_ref):
    total = None
    for i, score in enumerate(scores):
        weights = jnp.exp2((score - row_max) * SCALE2).astype(jnp.bfloat16)
        product = jnp.dot(weights, value_ref[i], preferred_element_type=jnp.float32)
        total = product if total is None else total + product
    return total


def near_kernel(row_ref, q_ref, own_ref, first_ref, second_ref, sum_ref, max_ref, bias_ref, value_ref):
    chunks = ((0, own_ref), (1, first_ref), (2, second_ref))
    tokens = bias_ref.shape[1]
    write_masks(row_ref[0], own_ref, chunks, bias_ref, value_ref)
    for head in range(RATIO):
        scores, row_max = masked_scores(q_ref, head, chunks, bias_ref)
        sum_ref[head] = weighted(scores, row_max, value_ref)
        max_ref[head] = jnp.broadcast_to(row_max, (tokens, DH))


def far_kernel(row_ref, q_ref, own_ref, third_ref, fourth_ref, sum_ref, max_ref, out_ref, *scratch_refs):
    bias_ref, value_ref, total_ref, top_ref = scratch_refs
    chunks = ((3, third_ref), (4, fourth_ref))
    count = q_ref.shape[1]
    tokens = count * COLS
    row = row_ref[0]
    last_doc = jnp.max(third_ref[tokens:, :].astype(jnp.float32))
    first_doc = jnp.min(own_ref[tokens:, :].astype(jnp.float32))
    wanted = (row >= 3) & (last_doc >= first_doc)
    lanes = lax.broadcasted_iota(jnp.int32, (tokens, DH), 1)

    def finish(head, total):
        denominator = total[:, DH:]
        mixed = (total[:, :DH] / denominator).astype(jnp.bfloat16)
        out_ref[:, head * count : (head + 1) * count, :] = mixed.reshape(COLS, count, DH)
        return denominator

    @pl.when(wanted)
    def _():
        write_masks(row, own_ref, chunks, bias_ref, value_ref)
        tops = jnp.zeros((tokens, DH), jnp.float32)
        sums = jnp.zeros((tokens, DH), jnp.float32)
        for head in range(RATIO):
            scores, row_max = masked_scores(q_ref, head, chunks, bias_ref)
            near_max = max_ref[head]
            row_max = jnp.maximum(near_max, row_max)
            decay = jnp.exp2((near_max - row_max) * SCALE2)
            total = sum_ref[head] * jnp.concatenate([decay, decay], 1)
            wide_max = jnp.concatenate([row_max, row_max], 1)
            denominator = finish(head, total + weighted(scores, wide_max, value_ref))
            mine = lanes % RATIO == head
            sums = jnp.where(mine, denominator, sums)
            tops = jnp.where(mine, row_max, tops)
        total_ref[...] = sums
        top_ref[...] = tops

    @pl.when(jnp.logical_not(wanted))
    def _():
        sums = jnp.zeros((tokens, DH), jnp.float32)
        tops = jnp.zeros((tokens, DH), jnp.float32)
        for head in range(RATIO):
            mine = lanes % RATIO == head
            sums = jnp.where(mine, finish(head, sum_ref[head]), sums)
            tops = jnp.where(mine, max_ref[head], tops)
        total_ref[...] = sums
        top_ref[...] = tops

    logs = top_ref[...] * SCALE + jnp.log(total_ref[...])
    high = logs.astype(jnp.bfloat16).astype(jnp.float32)
    logs = jnp.where(lanes < RATIO, high, logs - high).T[: 2 * RATIO]
    for step in range(COLS):
        piece = logs[:, step * count : (step + 1) * count]
        piece = jnp.concatenate([piece, piece], 1).astype(jnp.bfloat16)
        out_ref[step, RATIO * count :, :] = piece


def cost(tokens, count):
    return pl.CostEstimate(
        flops=6 * RATIO * tokens * tokens * count * DH,
        bytes_accessed=2 * 1024 * 1024,
        transcendentals=RATIO * tokens * tokens * count,
    )


def scratch(count, tokens):
    return [
        pltpu.VMEM((count, tokens, tokens), jnp.float32),
        pltpu.VMEM((count, tokens, 2 * DH), jnp.bfloat16),
    ]


def attend_near(row, query, own, first, second):
    tokens = query.shape[1] * COLS
    return pl.pallas_call(
        near_kernel,
        out_shape=[
            jax.ShapeDtypeStruct((RATIO, tokens, 2 * DH), jnp.float32),
            jax.ShapeDtypeStruct((RATIO, tokens, DH), jnp.float32),
        ],
        in_specs=[SMEM] + [VMEM] * 4,
        out_specs=[VMEM] * 2,
        scratch_shapes=scratch(3, tokens),
        compiler_params=params(),
        cost_estimate=cost(tokens, 3),
    )(row, query, own, first, second)


def attend_far(row, query, own, third, fourth, near):
    count = query.shape[1]
    tokens = count * COLS
    return pl.pallas_call(
        far_kernel,
        out_shape=jax.ShapeDtypeStruct((COLS, RATIO * count + 2 * RATIO, DH), jnp.bfloat16),
        in_specs=[SMEM] + [VMEM] * 6,
        out_specs=VMEM,
        scratch_shapes=scratch(2, tokens) + [pltpu.VMEM((tokens, DH), jnp.float32)] * 2,
        compiler_params=params(),
        cost_estimate=cost(tokens, 2),
    )(row, query, own, third, fourth, *near)


def join_kernel(in_ref, out_ref, log_ref):
    count = out_ref.shape[0]
    for home in range(COLS):
        for head in range(RATIO):
            first = (home * RATIO + head) * DH
            out_ref[:, first : first + DH] = in_ref[home, head * count : (head + 1) * count, :]
        logs = in_ref[home, RATIO * count :, :].astype(jnp.float32)
        logs = logs[:RATIO] + logs[RATIO:]
        log_ref[home * RATIO : (home + 1) * RATIO, :] = logs[:, :count]


def join(blocks, count):
    return pl.pallas_call(
        join_kernel,
        out_shape=[
            jax.ShapeDtypeStruct((count, QH * DH), jnp.bfloat16),
            jax.ShapeDtypeStruct((QH, count), jnp.float32),
        ],
        in_specs=[VMEM],
        out_specs=[VMEM] * 2,
        compiler_params=params(),
    )(blocks)


def per_device(queries, key_rows, value_rows, doc_ids):
    count = queries.shape[0]
    row = lax.axis_index("y").astype(jnp.int32)
    got = lax.all_to_all(pack(key_rows, value_rows, doc_ids), "z", 0, 0, tiled=True)
    own = jnp.concatenate(
        [piece[:count] for piece in got]
        + [jnp.concatenate([piece[count:, :count] for piece in got], 1)],
        0,
    )

    def ahead(array, back, least=0):
        return lax.ppermute(array, "y", [(i, i + back) for i in range(least, ROWS - back)])

    far = lax.ppermute(own, "y", [(i, (i + 6) % ROWS) for i in range(4)])
    chunks = [own] + [ahead(own, back) for back in (1, 2)]
    chunks.append(ahead(chunks[2], 1, 2))
    far = lax.ppermute(far, "y", [((i + 6) % ROWS, i + 4) for i in range(4)])
    chunks.append(far)

    query = jnp.transpose(queries.reshape(count, COLS, RATIO * DH), (1, 0, 2))
    query = lax.all_to_all(query, "z", 0, 0, tiled=True)
    own, first, second, third, fourth = chunks
    row = row.reshape(1)
    near = attend_near(row, query, own, first, second)
    blocks = attend_far(row, query, own, third, fourth, near)
    blocks = lax.all_to_all(blocks, "z", 0, 0, tiled=True)
    attended, log_totals = join(blocks, count)
    return attended, log_totals


def solution(mesh):
    names = ("grp", "y", "z")
    split_mesh = Mesh(mesh.devices.reshape(mesh.shape["grp"], ROWS, COLS), names)
    block = P(names, None)
    return jax.shard_map(
        per_device,
        mesh=split_mesh,
        in_specs=(block, block, block, P("grp", ("y", "z"))),
        out_specs=(block, P(None, names)),
        check_vma=False,
    )
```

```python
import functools
import math

import jax
import jax.numpy as jnp
from jax import lax
from jax.experimental import pallas as pl
from jax.experimental.pallas import tpu as pltpu
from jax.sharding import Mesh, PartitionSpec as P

QH = 32
KVH = 4
DH = 128
RATIO = QH // KVH
ROWS = 8
COLS = 4
NEG = -1e30
SCALE = 1.0 / math.sqrt(DH)
SCALE2 = SCALE * math.log2(math.e)
VMEM = pl.BlockSpec(memory_space=pltpu.VMEM)
SMEM = pl.BlockSpec(memory_space=pltpu.SMEM)
BACKWARD = [list(range(COLS))[::-1]]
ANY = pl.BlockSpec(memory_space=pl.ANY)


def params():
    return pltpu.CompilerParams(vmem_limit_bytes=40 * 1024 * 1024)


def pack_kernel(k_ref, v_ref, doc_ref, out_ref, line_ref, sems):
    count = k_ref.shape[0]
    copies = [pltpu.make_async_copy(doc_ref, line_ref, sems.at[0])]
    for head in range(COLS):
        part = slice(head * DH, (head + 1) * DH)
        for side, ref in enumerate((k_ref, v_ref)):
            target = out_ref.at[head, :count, side * DH : (side + 1) * DH]
            copies.append(pltpu.make_async_copy(ref.at[:, part], target, sems.at[1 + 2 * head + side]))
    for copy in copies:
        copy.start()
    copies[0].wait()
    docs = jnp.broadcast_to(line_ref[...].astype(jnp.float32), (16, count)).astype(jnp.bfloat16)
    for head in range(COLS):
        out_ref[head, count:, :] = jnp.zeros((16, 2 * DH), jnp.bfloat16)
        out_ref[head, count:, :count] = docs
    for copy in copies[1:]:
        copy.wait()


def pack(key_rows, value_rows, doc_ids):
    count = key_rows.shape[0]
    return pl.pallas_call(
        pack_kernel,
        out_shape=jax.ShapeDtypeStruct((COLS, count + 16, 2 * DH), jnp.bfloat16),
        in_specs=[ANY, ANY, ANY],
        out_specs=VMEM,
        scratch_shapes=[
            pltpu.VMEM(doc_ids.shape, doc_ids.dtype),
            pltpu.SemaphoreType.DMA((1 + 2 * COLS,)),
        ],
        compiler_params=pltpu.CompilerParams(vmem_limit_bytes=63 * 1024 * 1024),
    )(key_rows, value_rows, doc_ids)


def write_masks(row, own, chunks, bias_ref, value_ref):
    tokens = bias_ref.shape[1]
    doc_col = own[tokens:, :].astype(jnp.float32).T[:, :1]
    for i, (back, chunk) in enumerate(chunks):
        doc_row = chunk[tokens:, :].astype(jnp.float32)[:1]
        allowed = doc_col == doc_row
        if back == 0:
            q_pos = lax.broadcasted_iota(jnp.int32, (tokens, tokens), 0)
            k_pos = lax.broadcasted_iota(jnp.int32, (tokens, tokens), 1)
            allowed = allowed & (k_pos <= q_pos)
        else:
            allowed = allowed & (row >= back)
        bias_ref[i] = jnp.where(allowed, 0.0, NEG)
        value_ref[i, :, :DH] = chunk[:tokens, DH:]
        value_ref[i, :, DH:] = jnp.ones((tokens, DH), jnp.bfloat16)


def masked_scores(q_ref, head, chunks, bias_ref):
    tokens = bias_ref.shape[1]
    query = q_ref[:, :, head * DH : (head + 1) * DH].reshape(tokens, DH)
    scores = []
    for i, (_, chunk) in enumerate(chunks):
        product = lax.dot_general(
            query, chunk[:tokens, :DH], (((1,), (1,)), ((), ())), preferred_element_type=jnp.float32
        )
        scores.append(product + bias_ref[i])
    return scores, jnp.max(functools.reduce(jnp.maximum, scores), axis=1, keepdims=True)


def weighted(scores, row_max, value_ref):
    total = None
    for i, score in enumerate(scores):
        weights = jnp.exp2((score - row_max) * SCALE2).astype(jnp.bfloat16)
        product = jnp.dot(weights, value_ref[i], preferred_element_type=jnp.float32)
        total = product if total is None else total + product
    return total


def near_kernel(row_ref, q_ref, own_ref, first_ref, second_ref, sum_ref, max_ref, bias_ref, value_ref):
    chunks = ((0, own_ref), (1, first_ref), (2, second_ref))
    tokens = bias_ref.shape[1]
    write_masks(row_ref[0], own_ref, chunks, bias_ref, value_ref)
    for head in range(RATIO):
        scores, row_max = masked_scores(q_ref, head, chunks, bias_ref)
        sum_ref[head] = weighted(scores, row_max, value_ref)
        max_ref[head] = jnp.broadcast_to(row_max, (tokens, DH))


def far_kernel(row_ref, q_ref, own_ref, third_ref, fourth_ref, sum_ref, max_ref, out_ref, *scratch_refs):
    bias_ref, value_ref, total_ref, top_ref = scratch_refs
    chunks = ((3, third_ref), (4, fourth_ref))
    count = q_ref.shape[1]
    tokens = count * COLS
    row = row_ref[0]
    last_doc = jnp.max(third_ref[tokens:, :].astype(jnp.float32))
    first_doc = jnp.min(own_ref[tokens:, :].astype(jnp.float32))
    wanted = (row >= 3) & (last_doc >= first_doc)
    lanes = lax.broadcasted_iota(jnp.int32, (tokens, DH), 1)

    def finish(head, total):
        denominator = total[:, DH:]
        mixed = (total[:, :DH] / denominator).astype(jnp.bfloat16)
        for home in range(COLS):
            piece = mixed[home * count : (home + 1) * count]
            out_ref[COLS - 1 - home, head * count : (head + 1) * count, :] = piece
        return denominator

    @pl.when(wanted)
    def _():
        write_masks(row, own_ref, chunks, bias_ref, value_ref)
        tops = jnp.zeros((tokens, DH), jnp.float32)
        sums = jnp.zeros((tokens, DH), jnp.float32)
        for head in range(RATIO):
            scores, row_max = masked_scores(q_ref, head, chunks, bias_ref)
            near_max = max_ref[head]
            row_max = jnp.maximum(near_max, row_max)
            decay = jnp.exp2((near_max - row_max) * SCALE2)
            total = sum_ref[head] * jnp.concatenate([decay, decay], 1)
            wide_max = jnp.concatenate([row_max, row_max], 1)
            denominator = finish(head, total + weighted(scores, wide_max, value_ref))
            mine = lanes % RATIO == head
            sums = jnp.where(mine, denominator, sums)
            tops = jnp.where(mine, row_max, tops)
        total_ref[...] = sums
        top_ref[...] = tops

    @pl.when(jnp.logical_not(wanted))
    def _():
        sums = jnp.zeros((tokens, DH), jnp.float32)
        tops = jnp.zeros((tokens, DH), jnp.float32)
        for head in range(RATIO):
            mine = lanes % RATIO == head
            sums = jnp.where(mine, finish(head, sum_ref[head]), sums)
            tops = jnp.where(mine, max_ref[head], tops)
        total_ref[...] = sums
        top_ref[...] = tops

    logs = top_ref[...] * SCALE + jnp.log(total_ref[...])
    high = logs.astype(jnp.bfloat16).astype(jnp.float32)
    logs = jnp.where(lanes < RATIO, high, logs - high).T[: 2 * RATIO]
    for step in range(COLS):
        piece = logs[:, step * count : (step + 1) * count]
        piece = jnp.concatenate([piece, piece], 1).astype(jnp.bfloat16)
        out_ref[COLS - 1 - step, RATIO * count :, :] = piece


def cost(tokens, count):
    return pl.CostEstimate(
        flops=6 * RATIO * tokens * tokens * count * DH,
        bytes_accessed=2 * 1024 * 1024,
        transcendentals=RATIO * tokens * tokens * count,
    )


def scratch(count, tokens):
    return [
        pltpu.VMEM((count, tokens, tokens), jnp.float32),
        pltpu.VMEM((count, tokens, 2 * DH), jnp.bfloat16),
    ]


def attend_near(row, query, own, first, second):
    tokens = query.shape[1] * COLS
    return pl.pallas_call(
        near_kernel,
        out_shape=[
            jax.ShapeDtypeStruct((RATIO, tokens, 2 * DH), jnp.float32),
            jax.ShapeDtypeStruct((RATIO, tokens, DH), jnp.float32),
        ],
        in_specs=[SMEM] + [VMEM] * 4,
        out_specs=[VMEM] * 2,
        scratch_shapes=scratch(3, tokens),
        compiler_params=params(),
        cost_estimate=cost(tokens, 3),
    )(row, query, own, first, second)


def attend_far(row, query, own, third, fourth, near):
    count = query.shape[1]
    tokens = count * COLS
    return pl.pallas_call(
        far_kernel,
        out_shape=jax.ShapeDtypeStruct((COLS, RATIO * count + 2 * RATIO, DH), jnp.bfloat16),
        in_specs=[SMEM] + [VMEM] * 6,
        out_specs=VMEM,
        scratch_shapes=scratch(2, tokens) + [pltpu.VMEM((tokens, DH), jnp.float32)] * 2,
        compiler_params=params(),
        cost_estimate=cost(tokens, 2),
    )(row, query, own, third, fourth, *near)


def join_kernel(in_ref, out_ref, log_ref):
    count = out_ref.shape[0]
    for home in range(COLS):
        block_ref = in_ref.at[COLS - 1 - home]
        for head in range(RATIO):
            first = (home * RATIO + head) * DH
            out_ref[:, first : first + DH] = block_ref[head * count : (head + 1) * count, :]
        logs = block_ref[RATIO * count :, :].astype(jnp.float32)
        logs = logs[:RATIO] + logs[RATIO:]
        log_ref[home * RATIO : (home + 1) * RATIO, :] = logs[:, :count]


def join(blocks, count):
    return pl.pallas_call(
        join_kernel,
        out_shape=[
            jax.ShapeDtypeStruct((count, QH * DH), jnp.bfloat16),
            jax.ShapeDtypeStruct((QH, count), jnp.float32),
        ],
        in_specs=[VMEM],
        out_specs=[VMEM] * 2,
        compiler_params=params(),
    )(blocks)


def per_device(queries, key_rows, value_rows, doc_ids):
    count = queries.shape[0]
    row = lax.axis_index("y").astype(jnp.int32)
    got = lax.all_to_all(pack(key_rows, value_rows, doc_ids), "z", 0, 0, tiled=True)
    own = jnp.concatenate(
        [piece[:count] for piece in got]
        + [jnp.concatenate([piece[count:, :count] for piece in got], 1)],
        0,
    )

    def ahead(array, back, least=0):
        return lax.ppermute(array, "y", [(i, i + back) for i in range(least, ROWS - back)])

    far = lax.ppermute(own, "y", [(i, (i + 6) % ROWS) for i in range(4)])
    chunks = [own] + [ahead(own, back) for back in (1, 2)]
    chunks.append(ahead(chunks[2], 1, 2))
    far = lax.ppermute(far, "y", [((i + 6) % ROWS, i + 4) for i in range(4)])
    chunks.append(far)

    query = jnp.transpose(queries.reshape(count, COLS, RATIO * DH), (1, 0, 2))
    query = lax.all_to_all(query, "z", 0, 0, tiled=True)
    own, first, second, third, fourth = chunks
    row = row.reshape(1)
    near = attend_near(row, query, own, first, second)
    blocks = attend_far(row, query, own, third, fourth, near)
    blocks = lax.all_to_all(blocks, "z", 0, 0, tiled=True, axis_index_groups=BACKWARD)
    attended, log_totals = join(blocks, count)
    return attended, log_totals


def solution(mesh):
    names = ("grp", "y", "z")
    split_mesh = Mesh(mesh.devices.reshape(mesh.shape["grp"], ROWS, COLS), names)
    block = P(names, None)
    return jax.shard_map(
        per_device,
        mesh=split_mesh,
        in_specs=(block, block, block, P("grp", ("y", "z"))),
        out_specs=(block, P(None, names)),
        check_vma=False,
    )
```

```python
import functools
import math

import jax
import jax.numpy as jnp
from jax import lax
from jax.experimental import pallas as pl
from jax.experimental.pallas import tpu as pltpu
from jax.sharding import Mesh, PartitionSpec as P

QH = 32
KVH = 4
DH = 128
RATIO = QH // KVH
ROWS = 8
COLS = 4
NEG = -1e30
SCALE = 1.0 / math.sqrt(DH)
SCALE2 = SCALE * math.log2(math.e)
VMEM = pl.BlockSpec(memory_space=pltpu.VMEM)
SMEM = pl.BlockSpec(memory_space=pltpu.SMEM)
ORDER = (2, 3, 1, 0)
ANY = pl.BlockSpec(memory_space=pl.ANY)


def params():
    return pltpu.CompilerParams(vmem_limit_bytes=40 * 1024 * 1024)


def pack_kernel(k_ref, v_ref, doc_ref, out_ref, line_ref, sems):
    count = k_ref.shape[0]
    copies = [pltpu.make_async_copy(doc_ref, line_ref, sems.at[0])]
    for head in range(COLS):
        part = slice(head * DH, (head + 1) * DH)
        for side, ref in enumerate((k_ref, v_ref)):
            target = out_ref.at[head, :count, side * DH : (side + 1) * DH]
            copies.append(pltpu.make_async_copy(ref.at[:, part], target, sems.at[1 + 2 * head + side]))
    for copy in copies:
        copy.start()
    copies[0].wait()
    docs = jnp.broadcast_to(line_ref[...].astype(jnp.float32), (16, count)).astype(jnp.bfloat16)
    for head in range(COLS):
        out_ref[head, count:, :] = jnp.zeros((16, 2 * DH), jnp.bfloat16)
        out_ref[head, count:, :count] = docs
    for copy in copies[1:]:
        copy.wait()


def pack(key_rows, value_rows, doc_ids):
    count = key_rows.shape[0]
    return pl.pallas_call(
        pack_kernel,
        out_shape=jax.ShapeDtypeStruct((COLS, count + 16, 2 * DH), jnp.bfloat16),
        in_specs=[ANY, ANY, ANY],
        out_specs=VMEM,
        scratch_shapes=[
            pltpu.VMEM(doc_ids.shape, doc_ids.dtype),
            pltpu.SemaphoreType.DMA((1 + 2 * COLS,)),
        ],
        compiler_params=pltpu.CompilerParams(vmem_limit_bytes=63 * 1024 * 1024),
    )(key_rows, value_rows, doc_ids)


def write_masks(row, own, chunks, bias_ref, value_ref):
    tokens = bias_ref.shape[1]
    doc_col = own[tokens:, :].astype(jnp.float32).T[:, :1]
    for i, (back, chunk) in enumerate(chunks):
        doc_row = chunk[tokens:, :].astype(jnp.float32)[:1]
        allowed = doc_col == doc_row
        if back == 0:
            q_pos = lax.broadcasted_iota(jnp.int32, (tokens, tokens), 0)
            k_pos = lax.broadcasted_iota(jnp.int32, (tokens, tokens), 1)
            allowed = allowed & (k_pos <= q_pos)
        else:
            allowed = allowed & (row >= back)
        bias_ref[i] = jnp.where(allowed, 0.0, NEG)
        value_ref[i, :, :DH] = chunk[:tokens, DH:]
        value_ref[i, :, DH:] = jnp.ones((tokens, DH), jnp.bfloat16)


def masked_scores(q_ref, head, chunks, bias_ref):
    tokens = bias_ref.shape[1]
    query = q_ref[:, :, head * DH : (head + 1) * DH].reshape(tokens, DH)
    scores = []
    for i, (_, chunk) in enumerate(chunks):
        product = lax.dot_general(
            query, chunk[:tokens, :DH], (((1,), (1,)), ((), ())), preferred_element_type=jnp.float32
        )
        scores.append(product + bias_ref[i])
    return scores, jnp.max(functools.reduce(jnp.maximum, scores), axis=1, keepdims=True)


def weighted(scores, row_max, value_ref):
    total = None
    for i, score in enumerate(scores):
        weights = jnp.exp2((score - row_max) * SCALE2).astype(jnp.bfloat16)
        product = jnp.dot(weights, value_ref[i], preferred_element_type=jnp.float32)
        total = product if total is None else total + product
    return total


def near_kernel(row_ref, q_ref, own_ref, first_ref, second_ref, sum_ref, max_ref, bias_ref, value_ref):
    chunks = ((0, own_ref), (1, first_ref), (2, second_ref))
    tokens = bias_ref.shape[1]
    write_masks(row_ref[0], own_ref, chunks, bias_ref, value_ref)
    for head in range(RATIO):
        scores, row_max = masked_scores(q_ref, head, chunks, bias_ref)
        sum_ref[head] = weighted(scores, row_max, value_ref)
        max_ref[head] = jnp.broadcast_to(row_max, (tokens, DH))


def far_kernel(row_ref, q_ref, own_ref, third_ref, fourth_ref, sum_ref, max_ref, out_ref, *scratch_refs):
    bias_ref, value_ref, total_ref, top_ref = scratch_refs
    chunks = ((3, third_ref), (4, fourth_ref))
    count = q_ref.shape[1]
    tokens = count * COLS
    row = row_ref[0]
    last_doc = jnp.max(third_ref[tokens:, :].astype(jnp.float32))
    first_doc = jnp.min(own_ref[tokens:, :].astype(jnp.float32))
    wanted = (row >= 3) & (last_doc >= first_doc)
    lanes = lax.broadcasted_iota(jnp.int32, (tokens, DH), 1)

    def finish(head, total):
        denominator = total[:, DH:]
        mixed = (total[:, :DH] / denominator).astype(jnp.bfloat16)
        for home in range(COLS):
            piece = mixed[home * count : (home + 1) * count]
            out_ref[ORDER.index(home), head * count : (head + 1) * count, :] = piece
        return denominator

    @pl.when(wanted)
    def _():
        write_masks(row, own_ref, chunks, bias_ref, value_ref)
        tops = jnp.zeros((tokens, DH), jnp.float32)
        sums = jnp.zeros((tokens, DH), jnp.float32)
        for head in range(RATIO):
            scores, row_max = masked_scores(q_ref, head, chunks, bias_ref)
            near_max = max_ref[head]
            row_max = jnp.maximum(near_max, row_max)
            decay = jnp.exp2((near_max - row_max) * SCALE2)
            total = sum_ref[head] * jnp.concatenate([decay, decay], 1)
            wide_max = jnp.concatenate([row_max, row_max], 1)
            denominator = finish(head, total + weighted(scores, wide_max, value_ref))
            mine = lanes % RATIO == head
            sums = jnp.where(mine, denominator, sums)
            tops = jnp.where(mine, row_max, tops)
        total_ref[...] = sums
        top_ref[...] = tops

    @pl.when(jnp.logical_not(wanted))
    def _():
        sums = jnp.zeros((tokens, DH), jnp.float32)
        tops = jnp.zeros((tokens, DH), jnp.float32)
        for head in range(RATIO):
            mine = lanes % RATIO == head
            sums = jnp.where(mine, finish(head, sum_ref[head]), sums)
            tops = jnp.where(mine, max_ref[head], tops)
        total_ref[...] = sums
        top_ref[...] = tops

    logs = top_ref[...] * SCALE + jnp.log(total_ref[...])
    high = logs.astype(jnp.bfloat16).astype(jnp.float32)
    logs = jnp.where(lanes < RATIO, high, logs - high).T[: 2 * RATIO]
    for step in range(COLS):
        piece = logs[:, step * count : (step + 1) * count]
        piece = jnp.concatenate([piece, piece], 1).astype(jnp.bfloat16)
        out_ref[ORDER.index(step), RATIO * count :, :] = piece


def cost(tokens, count):
    return pl.CostEstimate(
        flops=6 * RATIO * tokens * tokens * count * DH,
        bytes_accessed=2 * 1024 * 1024,
        transcendentals=RATIO * tokens * tokens * count,
    )


def scratch(count, tokens):
    return [
        pltpu.VMEM((count, tokens, tokens), jnp.float32),
        pltpu.VMEM((count, tokens, 2 * DH), jnp.bfloat16),
    ]


def attend_near(row, query, own, first, second):
    tokens = query.shape[1] * COLS
    return pl.pallas_call(
        near_kernel,
        out_shape=[
            jax.ShapeDtypeStruct((RATIO, tokens, 2 * DH), jnp.float32),
            jax.ShapeDtypeStruct((RATIO, tokens, DH), jnp.float32),
        ],
        in_specs=[SMEM] + [VMEM] * 4,
        out_specs=[VMEM] * 2,
        scratch_shapes=scratch(3, tokens),
        compiler_params=params(),
        cost_estimate=cost(tokens, 3),
    )(row, query, own, first, second)


def attend_far(row, query, own, third, fourth, near):
    count = query.shape[1]
    tokens = count * COLS
    return pl.pallas_call(
        far_kernel,
        out_shape=jax.ShapeDtypeStruct((COLS, RATIO * count + 2 * RATIO, DH), jnp.bfloat16),
        in_specs=[SMEM] + [VMEM] * 6,
        out_specs=VMEM,
        scratch_shapes=scratch(2, tokens) + [pltpu.VMEM((tokens, DH), jnp.float32)] * 2,
        compiler_params=params(),
        cost_estimate=cost(tokens, 2),
    )(row, query, own, third, fourth, *near)


def join_kernel(in_ref, out_ref, log_ref):
    count = out_ref.shape[0]
    for home in range(COLS):
        block_ref = in_ref.at[ORDER.index(home)]
        for head in range(RATIO):
            first = (home * RATIO + head) * DH
            out_ref[:, first : first + DH] = block_ref[head * count : (head + 1) * count, :]
        logs = block_ref[RATIO * count :, :].astype(jnp.float32)
        logs = logs[:RATIO] + logs[RATIO:]
        log_ref[home * RATIO : (home + 1) * RATIO, :] = logs[:, :count]


def join(blocks, count):
    return pl.pallas_call(
        join_kernel,
        out_shape=[
            jax.ShapeDtypeStruct((count, QH * DH), jnp.bfloat16),
            jax.ShapeDtypeStruct((QH, count), jnp.float32),
        ],
        in_specs=[VMEM],
        out_specs=[VMEM] * 2,
        compiler_params=params(),
    )(blocks)


def per_device(queries, key_rows, value_rows, doc_ids):
    count = queries.shape[0]
    row = lax.axis_index("y").astype(jnp.int32)
    got = lax.all_to_all(pack(key_rows, value_rows, doc_ids), "z", 0, 0, tiled=True)
    own = jnp.concatenate(
        [piece[:count] for piece in got]
        + [jnp.concatenate([piece[count:, :count] for piece in got], 1)],
        0,
    )

    def ahead(array, back, least=0):
        return lax.ppermute(array, "y", [(i, i + back) for i in range(least, ROWS - back)])

    far = lax.ppermute(own, "y", [(i, (i + 6) % ROWS) for i in range(4)])
    chunks = [own] + [ahead(own, back) for back in (1, 2)]
    chunks.append(ahead(chunks[2], 1, 2))
    far = lax.ppermute(far, "y", [((i + 6) % ROWS, i + 4) for i in range(4)])
    chunks.append(far)

    query = jnp.transpose(queries.reshape(count, COLS, RATIO * DH), (1, 0, 2))
    query = lax.all_to_all(query, "z", 0, 0, tiled=True)
    own, first, second, third, fourth = chunks
    row = row.reshape(1)
    near = attend_near(row, query, own, first, second)
    blocks = attend_far(row, query, own, third, fourth, near)
    blocks = lax.all_to_all(blocks, "z", 0, 0, tiled=True, axis_index_groups=[list(ORDER)])
    attended, log_totals = join(blocks, count)
    return attended, log_totals


def solution(mesh):
    names = ("grp", "y", "z")
    split_mesh = Mesh(mesh.devices.reshape(mesh.shape["grp"], ROWS, COLS), names)
    block = P(names, None)
    return jax.shard_map(
        per_device,
        mesh=split_mesh,
        in_specs=(block, block, block, P("grp", ("y", "z"))),
        out_specs=(block, P(None, names)),
        check_vma=False,
    )
```
